128 devices in a mesh: row: 8 (over z_lo, y), col: 16 (over x, z_hi, core).
Axes of the slice: x: 4, y: 4, z: 4 (z_hi: 2, z_lo: 2; z = z_hi * 2 + z_lo), core: 2. Of those that a mesh axis runs over, the one named last changes fastest.
Arguments:
- film_embeds: float32 [16384, 1024], P(('row', 'col')), may hold values from -120 to 120
- text_embeds: float32 [16384, 1024], P(('col', 'row')), may hold values from -150 to 150
- matched_text_index: int32 [16384], replicated, may hold values from 0 to 16383, as said below
- sharpness_factor: float32 [1], replicated, may hold values from 20 to 60
- affinity_offset: float32 [1], replicated, may hold values from -12 to -6
Outputs:
- clip_loss: float32 [16384], P(('row', 'col'))
- grad_videos: float32 [16384, 1024], P(('row', 'col'))
- grad_captions: float32 [16384, 1024], P(('col', 'row'))
The draws below stay inside these ranges and needn't reach their ends.
Inputs may be any that keep to these rules, and one draw needn't show every extreme that they name: `matched_text_index`: each caption is the positive of exactly one clip.
All inputs are finite; a program needn't handle non-finite values.
Results may differ from the reference program's by a relative error of at most 0.0037.
Values may be sent and summed in bfloat16 or wider, within the bound.
A program may use at most 128 MiB of HBM per device.

```python
import math
import jax
import jax.numpy as jnp
from jax import lax

D = 1024
ROWS_PER_DEVICE = 128
CLIPS = 16384
N_COL = 16


def pairing(key):
    return jax.random.permutation(jax.random.fold_in(key, 101), CLIPS).astype(jnp.int32)


def rough_noise(key, shape):
    values = jnp.clip(jax.random.normal(key, shape, jnp.float32), -4.0, 4.0)
    return values / D ** 0.5


def video_unit_vectors(key):
    device_groups = max(CLIPS // 16, 1)
    members = jax.random.randint(jax.random.fold_in(key, 102), (CLIPS,), 0, device_groups)
    centres = rough_noise(jax.random.fold_in(key, 103), (device_groups, D))
    noise = rough_noise(jax.random.fold_in(key, 104), (CLIPS, D))
    share = jax.random.uniform(jax.random.fold_in(key, 105), (CLIPS, 1), jnp.float32, 0.1, 0.4)
    directions = jnp.sqrt(share) * centres[members] + jnp.sqrt(1.0 - share) * noise
    return directions


def row_scales(key):
    logs = jax.random.uniform(key, (CLIPS, 1), jnp.float32, jnp.log(10.0), jnp.log(100.0))
    return jnp.exp(logs)


def draw_matched_text_index(key, part):
    return pairing(key)


def draw_film_embeds(key, part):
    directions = video_unit_vectors(key)
    return (directions * row_scales(jax.random.fold_in(key, 106))).astype(jnp.float32)


def draw_text_embeds(key, part):
    directions = video_unit_vectors(key)
    order = pairing(key)
    keep = jax.random.uniform(jax.random.fold_in(key, 107), (CLIPS, 1), jnp.float32, 0.2, 0.8)
    noise = rough_noise(jax.random.fold_in(key, 108), (CLIPS, D))
    by_clip = jnp.sqrt(keep) * directions + jnp.sqrt(1.0 - keep) * noise
    placed = jnp.zeros((CLIPS, D), jnp.float32).at[order].set(by_clip)
    return (placed * row_scales(jax.random.fold_in(key, 109))).astype(jnp.float32)


def setup_inputs(seed: int = 0) -> dict:
    key_list = jax.random.split(jax.random.key(seed), 6)
    return {
        "film_embeds": draw_film_embeds(jax.random.fold_in(key_list[5], 71), 0),
        "text_embeds": draw_text_embeds(jax.random.fold_in(key_list[5], 71), 0),
        "matched_text_index": draw_matched_text_index(jax.random.fold_in(key_list[5], 71), 0),
        "sharpness_factor": jnp.clip(jnp.exp(jax.random.uniform(key_list[3], (1,), jnp.float32, math.log(20.0), math.log(60.0))), 20.0, 60.0),
        "affinity_offset": jnp.clip(jax.random.uniform(key_list[4], (1,), jnp.float32, -12.0, -6.0), -12.0, -6.0),
    }


def normalize(embed):
    inverse = lax.rsqrt(lax.optimization_barrier(jnp.sum(embed * embed, axis=1, keepdims=True)) + 1e-06)
    return (embed * inverse, inverse)

def backward_norm(hat, inverse, grad_hat):
    return inverse * (grad_hat - hat * lax.optimization_barrier(jnp.sum(hat * grad_hat, axis=1, keepdims=True)))

def reference(film_embeds, text_embeds, matched_text_index, sharpness_factor, affinity_offset):
    vhat, vnorm = normalize(film_embeds)
    chat, cnorm = normalize(text_embeds)
    v16 = vhat.astype(jnp.bfloat16)
    c16 = chat.astype(jnp.bfloat16)
    similarity_multiplier = sharpness_factor[0]
    shift = affinity_offset[0]
    total = CLIPS
    block = ROWS_PER_DEVICE * N_COL
    count = total // block
    matching_text_indices = jnp.arange(total, dtype=jnp.int32)

    def step(acc, index):
        start = (index * block).astype(jnp.int32)
        vblock = lax.dynamic_slice_in_dim(v16, start, block, 0)
        lblock = lax.dynamic_slice_in_dim(matched_text_index, start, block, 0)
        logits = jnp.dot(vblock, c16.T, preferred_element_type=jnp.float32) * similarity_multiplier + shift
        match = lblock[:, None] == matching_text_indices[None, :]
        sign = jnp.where(match, 1.0, -1.0).astype(jnp.float32)
        losses = lax.optimization_barrier(jnp.sum(jax.nn.softplus(-sign * logits), axis=1))
        coef = (jax.nn.sigmoid(logits) - match.astype(jnp.float32)).astype(jnp.bfloat16)
        dv = similarity_multiplier * jnp.dot(coef, c16, preferred_element_type=jnp.float32)
        acc = acc + jnp.dot(coef.T, vblock, preferred_element_type=jnp.float32)
        return (acc, (losses, dv))
    init = jnp.zeros((total, film_embeds.shape[1]), jnp.float32)
    acc, (losses, dvs) = lax.scan(step, init, jnp.arange(count, dtype=jnp.int32))
    clip_loss = losses.reshape(total)
    dvhat = dvs.reshape(total, film_embeds.shape[1])
    dchat = similarity_multiplier * acc
    return (clip_loss, backward_norm(vhat, vnorm, dvhat), backward_norm(chat, cnorm, dchat))
```

```python
import functools

import jax
import jax.numpy as jnp
from jax import lax
from jax.experimental import pallas as pl
from jax.experimental.pallas import tpu as pltpu
from jax.sharding import PartitionSpec as P

D = 1024
ROWS = 128
HALF = 64
LOG2E = 1.4426950408889634
LN2 = 0.6931471805599453
MESH = pl.DeviceIdType.MESH
F32 = jnp.float32
BF16 = jnp.bfloat16

RING = (0, 1, 3, 2)
OWN, NEXT, PREV, FAR = 0, 1, 2, 3


def position():
    r, c = lax.axis_index("row"), lax.axis_index("col")
    y, zl = r % 4, r // 4
    core, zh, x = c % 2, (c // 2) % 2, c // 4
    return r, c, x, y, zl, zh, core


def ring_step(i):
    return (i * (i + 1) // 2) % 4


def kernel(
    film, text, labels, scale, shift, loss_out, gv_out, gc_out,
    v16, c16, ct, coef, logits, lab, losses,
    dv_own, dv_sib, dv_tx, dv_core, dv_far, dv_ring, dv_z, dv_ztx,
    dc, dc_tx, dc_far, dc_ring, dc_z,
    ls_core, ls_ring, ls_z, send_sem, recv_sem,
):
    r, c, x, y, zl, zh, core = position()

    def dev(dx=0, dz_hi=0, dcore=0, dy=0, dz_lo=0):
        cc = (((x + dx) % 4) * 2 + (zh + dz_hi) % 2) * 2 + (core + dcore) % 2
        rr = ((zl + dz_lo) % 2) * 4 + (y + dy) % 4
        return (rr, cc)

    x_next, x_prev, x_far = dev(dx=1), dev(dx=3), dev(dx=2)
    y_next, y_prev = dev(dy=1), dev(dy=3)
    z_hi, z_lo, sibling = dev(dz_hi=1), dev(dz_lo=1), dev(dcore=1)

    barrier = pltpu.get_barrier_semaphore()
    peers = (x_next, x_prev, x_far, y_next, y_prev, z_hi, z_lo, sibling)
    for peer in peers:
        pl.semaphore_signal(barrier, inc=1, device_id=peer, device_id_type=MESH)

    copies = []

    def send(src, dst, peer):
        i = len(copies)
        copy = pltpu.make_async_remote_copy(
            src_ref=src, dst_ref=dst, send_sem=send_sem.at[i], recv_sem=recv_sem.at[i],
            device_id=peer, device_id_type=MESH,
        )
        copies.append(copy)
        copy.start()
        return copy

    s = scale[0]
    b = shift[0]

    f = film[...]
    vnorm = lax.rsqrt(jnp.sum(f * f, axis=1, keepdims=True) + 1e-06)
    v16[0:ROWS, :] = (f * vnorm).astype(BF16)
    t = text[...]
    cnorm = lax.rsqrt(jnp.sum(t * t, axis=1, keepdims=True) + 1e-06)
    c16[0:ROWS, :] = (t * cnorm).astype(BF16)

    pl.semaphore_wait(barrier, len(peers))

    def vrow(slot, dk=0, lo=0, n=ROWS):
        return v16.at[pl.ds(slot * 2 * ROWS + dk * ROWS + lo, n), :]

    def crow(slot, lo=0, n=ROWS):
        return c16.at[pl.ds(slot * ROWS + lo, n), :]

    def gather_own(row, z, nxt, prv):
        g = {}
        g["PA"] = send(row(4 * z, lo=0, n=HALF), row(4 * z + PREV, lo=0, n=HALF), nxt)
        g["NA"] = send(row(4 * z, lo=0, n=HALF), row(4 * z + NEXT, lo=0, n=HALF), prv)
        g["PB"] = send(row(4 * z, lo=HALF, n=HALF), row(4 * z + PREV, lo=HALF, n=HALF), nxt)
        g["NB"] = send(row(4 * z, lo=HALF, n=HALF), row(4 * z + NEXT, lo=HALF, n=HALF), prv)
        return g

    def forward_a(row, z, g, nxt):
        g["PA"].wait_recv()
        g["FA"] = send(row(4 * z + PREV, lo=0, n=HALF), row(4 * z + FAR, lo=0, n=HALF), nxt)

    def forward_b(row, z, g, prv):
        g["NB"].wait_recv()
        g["FB"] = send(row(4 * z + NEXT, lo=HALF, n=HALF), row(4 * z + FAR, lo=HALF, n=HALF), prv)

    core_copy = {}

    def to_sibling(slot):
        core_copy[slot] = send(vrow(slot), vrow(slot, dk=1), sibling)

    v_zh = send(vrow(0), vrow(4), z_hi)
    gv0 = gather_own(vrow, 0, x_next, x_prev)
    gc0 = gather_own(crow, 0, y_next, y_prev)
    c_zl = send(crow(0), crow(4), z_lo)
    to_sibling(0)

    for p in range(8):
        dz, i = p // 4, p % 4
        for dk in range(2):
            block = r * 16 + (((x + RING[i]) % 4) * 2 + (zh + dz) % 2) * 2 + (core + dk) % 2
            lab[p, :, dk * ROWS : (dk + 1) * ROWS] = labels[pl.ds(block, 1), :]
    losses[...] = jnp.zeros_like(losses)

    def transpose_c(slot):
        ct[:, slot * ROWS : (slot + 1) * ROWS] = c16[slot * ROWS : (slot + 1) * ROWS, :].T

    scale2 = s * LOG2E
    shift2 = b * LOG2E
    CH = 32

    def act(p, q0, nq):
        logits[0 : nq * ROWS, :] = lax.dot_general(
            c16[q0 * ROWS : (q0 + nq) * ROWS, :], v16[pl.ds(pl.multiple_of(p * 256, 256), 256), :],
            (((1,), (1,)), ((), ())), preferred_element_type=F32,
        )
        ids = lax.broadcasted_iota(jnp.int32, (CH, 256), 0)

        def chunk(j, acc):
            q = q0 + j // (ROWS // CH)
            base = (
                (c * 8 + ((zl + q // 4) % 2) * 4 + (y + ring_step(q % 4)) % 4) * ROWS
                + (j % (ROWS // CH)) * CH
            )
            rows = pl.ds(pl.multiple_of(j * CH, CH), CH)
            match = (lab[p] - base) == ids
            sign = jnp.where(match, -1.0, 1.0).astype(F32)
            e = jnp.exp2((logits[rows, :] * scale2 + shift2) * sign)
            w = 1.0 + e
            inv = pl.reciprocal(w, full_range=False)
            part = jnp.log2(w) * LN2 + (e - (w - 1.0)) * inv
            coef[
                pl.ds(pl.multiple_of(q0 * ROWS + j * CH, CH), CH), pl.ds(pl.multiple_of(p * 256, 256), 256)
            ] = (sign * (e * inv)).astype(BF16)
            for k in range(CH // 8):
                acc = acc + part[k * 8 : (k + 1) * 8, :]
            return acc

        acc = lax.fori_loop(0, nq * (ROWS // CH), chunk, jnp.zeros((8, 256), F32), unroll=2)
        losses[p] = losses[p] + acc[:, 0:ROWS]
        losses[8 + p] = losses[8 + p] + acc[:, ROWS:]

    def act_many(p0, p1, q0, nq):
        def body(p, _):
            act(p, q0, nq)
            return 0

        lax.fori_loop(p0, p1, body, 0)

    transpose_c(0)
    forward_a(vrow, 0, gv0, x_next)
    forward_a(crow, 0, gc0, y_next)
    forward_b(vrow, 0, gv0, x_prev)
    forward_b(crow, 0, gc0, y_prev)
    gv0["NA"].wait_recv()
    to_sibling(NEXT)
    gv0["PB"].wait_recv()
    to_sibling(PREV)
    gc0["NA"].wait_recv()
    gc0["PB"].wait_recv()
    v_zh.wait_recv()
    gv1 = gather_own(vrow, 1, x_next, x_prev)
    to_sibling(4)
    c_zl.wait_recv()
    gc1 = gather_own(crow, 1, y_next, y_prev)
    gv0["FA"].wait_recv()
    gv0["FB"].wait_recv()
    to_sibling(FAR)
    gc0["FA"].wait_recv()
    gc0["FB"].wait_recv()
    for slot in (1, 2, 3, 4):
        transpose_c(slot)
    for slot in (0, 1, 2, 3):
        core_copy[slot].wait_recv()
    act_many(0, 2, 0, 5)
    forward_a(vrow, 1, gv1, x_next)
    forward_a(crow, 1, gc1, y_next)
    forward_b(vrow, 1, gv1, x_prev)
    forward_b(crow, 1, gc1, y_prev)
    act_many(2, 4, 0, 5)
    core_copy[4].wait_recv()
    act_many(4, 5, 0, 5)
    gv1["NA"].wait_recv()
    to_sibling(4 + NEXT)
    gv1["PB"].wait_recv()
    to_sibling(4 + PREV)
    gc1["NA"].wait_recv()
    gc1["PB"].wait_recv()
    transpose_c(5)
    transpose_c(6)
    core_copy[5].wait_recv()
    core_copy[6].wait_recv()
    act_many(0, 5, 5, 2)
    act_many(5, 7, 0, 7)
    gv1["FA"].wait_recv()
    gv1["FB"].wait_recv()
    to_sibling(4 + FAR)
    gc1["FA"].wait_recv()
    gc1["FB"].wait_recv()
    transpose_c(7)
    act_many(0, 7, 7, 1)
    core_copy[7].wait_recv()
    act_many(7, 8, 0, 8)

    ls_copy_core = send(losses.at[pl.ds(8, 8)], ls_core, sibling)

    dv_core_copy = {}

    def make_dv(p):
        for m in range(2):
            rows = slice(m * 512, (m + 1) * 512)
            out = jnp.dot(ct[rows, :], coef[:, p * 256 : (p + 1) * 256], preferred_element_type=F32)
            dv_own[p, rows, :] = out[:, 0:ROWS]
            dv_sib[p, rows, :] = out[:, ROWS:].astype(BF16)
        dv_core_copy[p] = send(dv_sib.at[p], dv_core.at[p], sibling)

    def make_dc(qa, qb):
        left = jnp.concatenate(
            [coef[qa * ROWS : (qa + 1) * ROWS, :], coef[qb * ROWS : (qb + 1) * ROWS, :]], axis=0
        )

        def body(n, _):
            cols = pl.ds(pl.multiple_of(n * 256, 256), 256)
            out = jnp.dot(left, v16[:, cols], preferred_element_type=F32)
            dc[qa, :, cols] = out[0:ROWS]
            dc[qb, :, cols] = out[ROWS:]
            return 0

        lax.fori_loop(0, 4, body, 0)

    dv_far_copy, dv_ring_copy, dc_far_copy, dc_ring_copy = {}, {}, {}, {}

    def dv_send_far(z):
        p = 4 * z + FAR
        dv_core_copy[p].wait_recv()
        dv_tx[p] = (dv_own[p] + dv_core[p].astype(F32)).astype(BF16)
        dv_far_copy[z, 0] = send(dv_tx.at[p, pl.ds(0, 512)], dv_far.at[z, pl.ds(0, 512)], x_next)
        dv_far_copy[z, 1] = send(dv_tx.at[p, pl.ds(512, 512)], dv_far.at[z, pl.ds(512, 512)], x_prev)

    def dv_send_free(z):
        for i, peer, k in ((NEXT, x_next, 1), (PREV, x_prev, 0)):
            p = 4 * z + i
            dv_core_copy[p].wait_recv()
            half = pl.ds(512 * k, 512)
            dv_tx[p, half, :] = (dv_own[p, half, :] + dv_core[p, half, :].astype(F32)).astype(BF16)
            dv_ring_copy[z, i, k] = send(dv_tx.at[p, half], dv_ring.at[2 * z + i - 1, half], peer)

    def dv_send_rest(z):
        for i, peer, k in ((NEXT, x_next, 0), (PREV, x_prev, 1)):
            p = 4 * z + i
            half = pl.ds(512 * k, 512)
            dv_far_copy[z, k].wait_recv()
            dv_tx[p, half, :] = (
                dv_own[p, half, :] + dv_core[p, half, :].astype(F32) + dv_far[z, half, :].astype(F32)
            ).astype(BF16)
            dv_ring_copy[z, i, k] = send(dv_tx.at[p, half], dv_ring.at[2 * z + i - 1, half], peer)

    def dv_total(z):
        p = 4 * z
        dv_core_copy[p].wait_recv()
        for i in (NEXT, PREV):
            for k in range(2):
                dv_ring_copy[z, i, k].wait_recv()
        return (
            dv_own[p] + dv_core[p].astype(F32)
            + (dv_ring[2 * z].astype(F32) + dv_ring[2 * z + 1].astype(F32))
        )

    def dc_send_far(z):
        q = 4 * z + FAR
        dc_tx[q] = dc[q].astype(BF16)
        dc_far_copy[z, 0] = send(dc_tx.at[q, pl.ds(0, HALF)], dc_far.at[z, pl.ds(0, HALF)], y_next)
        dc_far_copy[z, 1] = send(dc_tx.at[q, pl.ds(HALF, HALF)], dc_far.at[z, pl.ds(HALF, HALF)], y_prev)

    def dc_send_free(z):
        for i, peer, k in ((NEXT, y_next, 1), (PREV, y_prev, 0)):
            q = 4 * z + i
            half = pl.ds(HALF * k, HALF)
            dc_tx[q, half, :] = dc[q, half, :].astype(BF16)
            dc_ring_copy[z, i, k] = send(dc_tx.at[q, half], dc_ring.at[2 * z + i - 1, half], peer)

    def dc_send_rest(z):
        for i, peer, k in ((NEXT, y_next, 0), (PREV, y_prev, 1)):
            q = 4 * z + i
            half = pl.ds(HALF * k, HALF)
            dc_far_copy[z, k].wait_recv()
            dc_tx[q, half, :] = (dc[q, half, :] + dc_far[z, half, :].astype(F32)).astype(BF16)
            dc_ring_copy[z, i, k] = send(dc_tx.at[q, half], dc_ring.at[2 * z + i - 1, half], peer)

    def dc_total(z):
        for i in (NEXT, PREV):
            for k in range(2):
                dc_ring_copy[z, i, k].wait_recv()
        return dc[4 * z] + (dc_ring[2 * z].astype(F32) + dc_ring[2 * z + 1].astype(F32))

    make_dv(7)
    make_dv(3)
    make_dc(7, 3)
    dc_send_far(1)
    dc_send_far(0)
    dv_send_far(1)
    dv_send_far(0)
    ls_copy_core.wait_recv()
    for p in range(8):
        losses[p] = losses[p] + ls_core[p]
    ls_copies = []
    for i, peer in ((NEXT, x_next), (PREV, x_prev), (FAR, x_far)):
        for z in range(2):
            ls_copies.append(send(losses.at[4 * z + i], ls_ring.at[3 * z + i - 1], peer))
    make_dv(5)
    make_dv(6)
    make_dc(5, 6)
    dc_send_free(1)
    dv_send_free(1)
    make_dc(1, 2)
    dc_send_rest(1)
    dv_send_rest(1)
    dc_send_free(0)
    make_dv(1)
    make_dv(2)
    dv_send_free(0)
    dc_send_rest(0)
    dv_send_rest(0)
    make_dc(4, 0)
    make_dv(4)
    make_dv(0)
    for copy in ls_copies:
        copy.wait_recv()
    losses[4] = losses[4] + (ls_ring[3] + ls_ring[4] + ls_ring[5])
    losses[0] = losses[0] + (ls_ring[0] + ls_ring[1] + ls_ring[2])
    ls_copy_z = send(losses.at[4], ls_z, z_hi)
    dc_tx[4] = dc_total(1).astype(BF16)
    dc_copy_z = send(dc_tx.at[4], dc_z, z_lo)
    dv_ztx[...] = dv_total(1).astype(BF16)
    dv_copy_z = send(dv_ztx, dv_z, z_hi)

    ls_copy_z.wait_recv()
    loss_out[...] = jnp.sum(losses[0] + ls_z[...], axis=0, keepdims=True)

    total = dc_total(0)
    dc_copy_z.wait_recv()
    dchat = s * (total + dc_z[...].astype(F32))
    chat = text[...] * cnorm
    gc_out[...] = cnorm * (dchat - chat * jnp.sum(chat * dchat, axis=1, keepdims=True))

    total = dv_total(0)
    dv_copy_z.wait_recv()
    dvhat = s * (total + dv_z[...].astype(F32)).T
    vhat = film[...] * vnorm
    gv_out[...] = vnorm * (dvhat - vhat * jnp.sum(vhat * dvhat, axis=1, keepdims=True))

    for copy in copies:
        copy.wait_send()


N_COPIES = 76


def shards(film, text, matched, scale, shift):
    vmem = pl.BlockSpec(memory_space=pltpu.VMEM)
    smem = pl.BlockSpec(memory_space=pltpu.SMEM)
    loss, gv, gc = pl.pallas_call(
        kernel,
        out_shape=(
            jax.ShapeDtypeStruct((1, ROWS), F32),
            jax.ShapeDtypeStruct((ROWS, D), F32),
            jax.ShapeDtypeStruct((ROWS, D), F32),
        ),
        in_specs=[vmem, vmem, vmem, smem, smem],
        out_specs=(vmem, vmem, vmem),
        scratch_shapes=[
            pltpu.VMEM((2048, D), BF16),
            pltpu.VMEM((1024, D), BF16),
            pltpu.VMEM((D, 1024), BF16),
            pltpu.VMEM((1024, 2048), BF16),
            pltpu.VMEM((1024, 256), F32),
            pltpu.VMEM((8, 1, 256), jnp.int32),
            pltpu.VMEM((16, 8, ROWS), F32),
            pltpu.VMEM((8, D, ROWS), F32),
            pltpu.VMEM((8, D, ROWS), BF16),
            pltpu.VMEM((8, D, ROWS), BF16),
            pltpu.VMEM((8, D, ROWS), BF16),
            pltpu.VMEM((2, D, ROWS), BF16),
            pltpu.VMEM((4, D, ROWS), BF16),
            pltpu.VMEM((D, ROWS), BF16),
            pltpu.VMEM((D, ROWS), BF16),
            pltpu.VMEM((8, ROWS, D), F32),
            pltpu.VMEM((8, ROWS, D), BF16),
            pltpu.VMEM((2, ROWS, D), BF16),
            pltpu.VMEM((4, ROWS, D), BF16),
            pltpu.VMEM((ROWS, D), BF16),
            pltpu.VMEM((8, 8, ROWS), F32),
            pltpu.VMEM((6, 8, ROWS), F32),
            pltpu.VMEM((8, ROWS), F32),
            pltpu.SemaphoreType.DMA((N_COPIES,)),
            pltpu.SemaphoreType.DMA((N_COPIES,)),
        ],
        compiler_params=pltpu.CompilerParams(
            collective_id=0, has_side_effects=True, vmem_limit_bytes=60 * 2**20
        ),
        cost_estimate=pl.CostEstimate(flops=13 * 10**9, bytes_accessed=2 * 2**20, transcendentals=0),
    )(film, text, matched.reshape(ROWS, ROWS), scale, shift)
    return loss.reshape(ROWS), gv, gc


def solution(mesh):
    return jax.shard_map(
        shards,
        mesh=mesh,
        in_specs=(P(("row", "col"), None), P(("col", "row"), None), P(), P(), P()),
        out_specs=(P(("row", "col")), P(("row", "col"), None), P(("col", "row"), None)),
        check_vma=False,
    )
```

```python
import functools

import jax
import jax.numpy as jnp
from jax import lax
from jax.experimental import pallas as pl
from jax.experimental.pallas import tpu as pltpu
from jax.sharding import PartitionSpec as P

D = 1024
ROWS = 128
HALF = 64
CH = 32
LOG2E = 1.4426950408889634
LN2 = 0.6931471805599453
MESH = pl.DeviceIdType.MESH
F32 = jnp.float32
BF16 = jnp.bfloat16

RING = (0, 1, 3, 2)
OWN, NEXT, PREV, FAR = 0, 1, 2, 3


def position():
    r, c = lax.axis_index("row"), lax.axis_index("col")
    y, zl = r % 4, r // 4
    core, zh, x = c % 2, (c // 2) % 2, c // 4
    return r, c, x, y, zl, zh, core


def kernel(
    film_in, text_in, labels_in, scale_in, shift_in, loss_out, gv_out, gc_out,
    film, text, labels, scale, shift, gv, gc, v16, c16, ct, coef, logits, lab, base, losses,
    dv_own, dv_sib, dv_tx, dv_core, dv_far, dv_ring, dv_z, dv_ztx,
    dc, dc_tx, dc_far, dc_ring, dc_z,
    ls_core, ls_ring, ls_z, send_sem, recv_sem, io_sem,
):
    r, c, x, y, zl, zh, core = position()

    def dev(dx=0, dz_hi=0, dcore=0, dy=0, dz_lo=0):
        cc = (((x + dx) % 4) * 2 + (zh + dz_hi) % 2) * 2 + (core + dcore) % 2
        rr = ((zl + dz_lo) % 2) * 4 + (y + dy) % 4
        return (rr, cc)

    x_next, x_prev, x_far = dev(dx=1), dev(dx=3), dev(dx=2)
    y_next, y_prev = dev(dy=1), dev(dy=3)
    z_hi, z_lo, sibling = dev(dz_hi=1), dev(dz_lo=1), dev(dcore=1)

    barrier = pltpu.get_barrier_semaphore()
    peers = (x_next, x_prev, x_far, y_next, y_prev, z_hi, z_lo, sibling)
    for peer in peers:
        pl.semaphore_signal(barrier, inc=1, device_id=peer, device_id_type=MESH)

    loads = [
        pltpu.make_async_copy(src, dst, io_sem.at[i])
        for i, (src, dst) in enumerate((
            (film_in, film), (text_in, text), (labels_in, labels), (scale_in, scale), (shift_in, shift)
        ))
    ]
    for load in loads:
        load.start()

    copies, sent = [], []

    def send(src, dst, peer):
        i = len(copies)
        copy = pltpu.make_async_remote_copy(
            src_ref=src, dst_ref=dst, send_sem=send_sem.at[i], recv_sem=recv_sem.at[i],
            device_id=peer, device_id_type=MESH,
        )
        copies.append(copy)
        copy.start()
        return copy

    loads[0].wait()
    f = film[...]
    vnorm = lax.rsqrt(jnp.sum(f * f, axis=1, keepdims=True) + 1e-06)
    v16[0:ROWS, :] = (f * vnorm).astype(BF16)
    loads[1].wait()
    t = text[...]
    cnorm = lax.rsqrt(jnp.sum(t * t, axis=1, keepdims=True) + 1e-06)
    c16[0:ROWS, :] = (t * cnorm).astype(BF16)

    pl.semaphore_wait(barrier, len(peers))

    def vrow(slot, dk=0, lo=0, n=ROWS):
        return v16.at[pl.ds(slot * 2 * ROWS + dk * ROWS + lo, n), :]

    def crow(slot, lo=0, n=ROWS):
        return c16.at[pl.ds(slot * ROWS + lo, n), :]

    def gather_first(row, z, nxt, prv):
        return {
            "PA": send(row(4 * z, lo=0, n=HALF), row(4 * z + PREV, lo=0, n=HALF), nxt),
            "NB": send(row(4 * z, lo=HALF, n=HALF), row(4 * z + NEXT, lo=HALF, n=HALF), prv),
        }

    def gather_second(row, z, g, nxt, prv):
        g["PA"].wait_send()
        g["PB"] = send(row(4 * z, lo=HALF, n=HALF), row(4 * z + PREV, lo=HALF, n=HALF), nxt)
        g["NB"].wait_send()
        g["NA"] = send(row(4 * z, lo=0, n=HALF), row(4 * z + NEXT, lo=0, n=HALF), prv)
        sent.extend((g["PA"], g["NB"]))

    def forward(row, z, g, nxt, prv):
        g["PA"].wait_recv()
        g["FA"] = send(row(4 * z + PREV, lo=0, n=HALF), row(4 * z + FAR, lo=0, n=HALF), nxt)
        g["NB"].wait_recv()
        g["FB"] = send(row(4 * z + NEXT, lo=HALF, n=HALF), row(4 * z + FAR, lo=HALF, n=HALF), prv)

    core_copy = {}

    def to_sibling(slot):
        core_copy[slot] = send(vrow(slot), vrow(slot, dk=1), sibling)

    v_zh = send(vrow(0), vrow(4), z_hi)
    gv0 = gather_first(vrow, 0, x_next, x_prev)
    gc0 = gather_first(crow, 0, y_next, y_prev)
    to_sibling(0)

    for load in loads[2:]:
        load.wait()
    s = scale[0]
    b = shift[0]
    for p in range(8):
        dz, i = p // 4, p % 4
        for dk in range(2):
            block = r * 16 + (((x + RING[i]) % 4) * 2 + (zh + dz) % 2) * 2 + (core + dk) % 2
            lab[p, :, dk * ROWS : (dk + 1) * ROWS] = labels[pl.ds(block, 1), :]
        base[p] = (c * 8 + ((zl + dz) % 2) * 4 + (y + RING[i]) % 4) * ROWS
    losses[...] = jnp.zeros_like(losses)

    def transpose_c(slot):
        ct[:, slot * ROWS : (slot + 1) * ROWS] = c16[slot * ROWS : (slot + 1) * ROWS, :].T

    scale2 = s * LOG2E
    shift2 = b * LOG2E

    def act_many(p0, p1, q0, nq):
        left = c16[q0 * ROWS : (q0 + nq) * ROWS, :]
        for p in range(p0, p1):
            logits[p, 0 : nq * ROWS, :] = lax.dot_general(
                left, v16[p * 256 : (p + 1) * 256, :], (((1,), (1,)), ((), ())), preferred_element_type=F32
            )
        ids = lax.broadcasted_iota(jnp.int32, (CH, 256), 0)

        def pair(p, _):
            cols = pl.ds(pl.multiple_of(p * 256, 256), 256)

            def shard(k, acc):
                mine = lab[p] - base[q0 + k]
                for j in range(ROWS // CH):
                    sign = jnp.where((mine - j * CH) == ids, -1.0, 1.0).astype(F32)
                    rows = pl.ds(pl.multiple_of(k * ROWS + j * CH, CH), CH)
                    e = jnp.exp2((logits[p, rows, :] * scale2 + shift2) * sign)
                    w = 1.0 + e
                    inv = pltpu.reciprocal(w, full_range=False)
                    part = jnp.log2(w) * LN2 + (e - (w - 1.0)) * inv
                    coef[pl.ds(pl.multiple_of((q0 + k) * ROWS + j * CH, CH), CH), cols] = (
                        sign * (e * inv)
                    ).astype(BF16)
                    for i in range(CH // 8):
                        acc = acc + part[i * 8 : (i + 1) * 8, :]
                return acc

            acc = jnp.zeros((8, 256), F32)
            acc = shard(0, acc) if nq == 1 else lax.fori_loop(0, nq, shard, acc)
            losses[p] = losses[p] + acc[:, 0:ROWS]
            losses[8 + p] = losses[8 + p] + acc[:, ROWS:]
            return 0

        lax.fori_loop(p0, p1, pair, 0)

    transpose_c(0)
    core_copy[0].wait_recv()
    act_many(0, 1, 0, 1)
    gather_second(vrow, 0, gv0, x_next, x_prev)
    gather_second(crow, 0, gc0, y_next, y_prev)
    forward(vrow, 0, gv0, x_next, x_prev)
    forward(crow, 0, gc0, y_next, y_prev)
    v_zh.wait_send()
    sent.append(v_zh)
    c_zl = send(crow(0), crow(4), z_lo)
    v_zh.wait_recv()
    gv1 = gather_first(vrow, 1, x_next, x_prev)
    to_sibling(4)
    gv0["NA"].wait_recv()
    to_sibling(NEXT)
    gv0["PB"].wait_recv()
    to_sibling(PREV)
    gc0["NA"].wait_recv()
    gc0["PB"].wait_recv()
    transpose_c(1)
    transpose_c(2)
    act_many(0, 1, 1, 2)
    core_copy[1].wait_recv()
    core_copy[2].wait_recv()
    act_many(1, 3, 0, 3)
    gather_second(vrow, 1, gv1, x_next, x_prev)
    gv0["FA"].wait_recv()
    gv0["FB"].wait_recv()
    to_sibling(FAR)
    gc0["FA"].wait_recv()
    gc0["FB"].wait_recv()
    transpose_c(3)
    act_many(0, 3, 3, 1)
    c_zl.wait_recv()
    gc1 = gather_first(crow, 1, y_next, y_prev)
    forward(vrow, 1, gv1, x_next, x_prev)
    core_copy[3].wait_recv()
    core_copy[4].wait_recv()
    act_many(3, 5, 0, 4)
    transpose_c(4)
    act_many(0, 5, 4, 1)
    gather_second(crow, 1, gc1, y_next, y_prev)
    gv1["NA"].wait_recv()
    to_sibling(4 + NEXT)
    gv1["PB"].wait_recv()
    to_sibling(4 + PREV)
    forward(crow, 1, gc1, y_next, y_prev)
    core_copy[5].wait_recv()
    core_copy[6].wait_recv()
    act_many(5, 7, 0, 5)
    gv1["FA"].wait_recv()
    gv1["FB"].wait_recv()
    to_sibling(4 + FAR)
    gc1["NA"].wait_recv()
    gc1["PB"].wait_recv()
    transpose_c(5)
    transpose_c(6)
    act_many(0, 7, 5, 2)
    core_copy[7].wait_recv()
    act_many(7, 8, 0, 7)
    gc1["FA"].wait_recv()
    gc1["FB"].wait_recv()
    transpose_c(7)
    act_many(0, 8, 7, 1)

    ls_copy_core = send(losses.at[pl.ds(8, 8)], ls_core, sibling)

    dv_core_copy = {}

    def make_dv(p):
        for m in range(2):
            rows = slice(m * 512, (m + 1) * 512)
            out = jnp.dot(ct[rows, :], coef[:, p * 256 : (p + 1) * 256], preferred_element_type=F32)
            dv_own[p, rows, :] = out[:, 0:ROWS]
            dv_sib[p, rows, :] = out[:, ROWS:].astype(BF16)
        dv_core_copy[p] = send(dv_sib.at[p], dv_core.at[p], sibling)

    def make_dc(q):
        def body(n, _):
            cols = pl.ds(pl.multiple_of(n * 512, 512), 512)
            dc[q, :, cols] = jnp.dot(
                coef[q * ROWS : (q + 1) * ROWS, :], v16[:, cols], preferred_element_type=F32
            )
            return 0

        lax.fori_loop(0, 2, body, 0)

    dv_far_copy, dv_ring_copy, dc_far_copy, dc_ring_copy = {}, {}, {}, {}

    def dv_send_far(z):
        p = 4 * z + FAR
        dv_core_copy[p].wait_recv()
        dv_tx[p] = (dv_own[p] + dv_core[p].astype(F32)).astype(BF16)
        dv_far_copy[z, 0] = send(dv_tx.at[p, pl.ds(0, 512)], dv_far.at[z, pl.ds(0, 512)], x_next)
        dv_far_copy[z, 1] = send(dv_tx.at[p, pl.ds(512, 512)], dv_far.at[z, pl.ds(512, 512)], x_prev)

    def dv_send_free(z):
        for i, peer, k in ((NEXT, x_next, 1), (PREV, x_prev, 0)):
            p = 4 * z + i
            dv_core_copy[p].wait_recv()
            half = pl.ds(512 * k, 512)
            dv_tx[p, half, :] = (dv_own[p, half, :] + dv_core[p, half, :].astype(F32)).astype(BF16)
            dv_ring_copy[z, i, k] = send(dv_tx.at[p, half], dv_ring.at[2 * z + i - 1, half], peer)

    def dv_send_rest(z):
        for i, peer, k in ((NEXT, x_next, 0), (PREV, x_prev, 1)):
            p = 4 * z + i
            half = pl.ds(512 * k, 512)
            dv_far_copy[z, k].wait_recv()
            dv_tx[p, half, :] = (
                dv_own[p, half, :] + dv_core[p, half, :].astype(F32) + dv_far[z, half, :].astype(F32)
            ).astype(BF16)
            dv_ring_copy[z, i, k] = send(dv_tx.at[p, half], dv_ring.at[2 * z + i - 1, half], peer)

    def dv_total(z):
        p = 4 * z
        dv_core_copy[p].wait_recv()
        for i in (NEXT, PREV):
            for k in range(2):
                dv_ring_copy[z, i, k].wait_recv()
        return (
            dv_own[p] + dv_core[p].astype(F32)
            + (dv_ring[2 * z].astype(F32) + dv_ring[2 * z + 1].astype(F32))
        )

    def dc_send_far(z):
        q = 4 * z + FAR
        dc_tx[q] = dc[q].astype(BF16)
        dc_far_copy[z, 0] = send(dc_tx.at[q, pl.ds(0, HALF)], dc_far.at[z, pl.ds(0, HALF)], y_next)
        dc_far_copy[z, 1] = send(dc_tx.at[q, pl.ds(HALF, HALF)], dc_far.at[z, pl.ds(HALF, HALF)], y_prev)

    def dc_send_free(z):
        for i, peer, k in ((NEXT, y_next, 1), (PREV, y_prev, 0)):
            q = 4 * z + i
            half = pl.ds(HALF * k, HALF)
            dc_tx[q, half, :] = dc[q, half, :].astype(BF16)
            dc_ring_copy[z, i, k] = send(dc_tx.at[q, half], dc_ring.at[2 * z + i - 1, half], peer)

    def dc_send_rest(z):
        for i, peer, k in ((NEXT, y_next, 0), (PREV, y_prev, 1)):
            q = 4 * z + i
            half = pl.ds(HALF * k, HALF)
            dc_far_copy[z, k].wait_recv()
            dc_tx[q, half, :] = (dc[q, half, :] + dc_far[z, half, :].astype(F32)).astype(BF16)
            dc_ring_copy[z, i, k] = send(dc_tx.at[q, half], dc_ring.at[2 * z + i - 1, half], peer)

    def dc_total(z):
        for i in (NEXT, PREV):
            for k in range(2):
                dc_ring_copy[z, i, k].wait_recv()
        return dc[4 * z] + (dc_ring[2 * z].astype(F32) + dc_ring[2 * z + 1].astype(F32))

    make_dv(7)
    make_dc(7)
    dc_send_far(1)
    make_dv(5)
    dv_send_far(1)
    make_dv(6)
    make_dc(5)
    make_dc(6)
    dc_send_free(1)
    dv_send_free(1)
    ls_copy_core.wait_recv()
    for p in range(8):
        losses[p] = losses[p] + ls_core[p]
    ls_copies = []
    for i, peer in ((NEXT, x_next), (PREV, x_prev), (FAR, x_far)):
        for z in range(2):
            ls_copies.append(send(losses.at[4 * z + i], ls_ring.at[3 * z + i - 1], peer))
    make_dc(4)
    make_dv(4)
    dc_send_rest(1)
    dv_send_rest(1)
    make_dc(3)
    make_dv(3)
    dc_send_far(0)
    make_dc(1)
    make_dc(2)
    dv_send_far(0)
    dc_tx[4] = dc_total(1).astype(BF16)
    dc_copy_z = send(dc_tx.at[4], dc_z, z_lo)
    dv_ztx[...] = dv_total(1).astype(BF16)
    dv_copy_z = send(dv_ztx, dv_z, z_hi)
    make_dv(1)
    make_dv(2)
    dc_send_free(0)
    dv_send_free(0)
    dc_send_rest(0)
    dv_send_rest(0)
    make_dc(0)
    make_dv(0)
    for copy in ls_copies:
        copy.wait_recv()
    losses[4] = losses[4] + (ls_ring[3] + ls_ring[4] + ls_ring[5])
    losses[0] = losses[0] + (ls_ring[0] + ls_ring[1] + ls_ring[2])
    ls_copy_z = send(losses.at[4], ls_z, z_hi)
    ls_copy_z.wait_recv()
    loss_out[...] = jnp.sum(losses[0] + ls_z[...], axis=0, keepdims=True)

    total = dc_total(0)
    dc_copy_z.wait_recv()
    dchat = s * (total + dc_z[...].astype(F32))
    chat = text[...] * cnorm
    gc[...] = cnorm * (dchat - chat * jnp.sum(chat * dchat, axis=1, keepdims=True))

    gc_store = pltpu.make_async_copy(gc, gc_out, io_sem.at[0])
    gc_store.start()

    total = dv_total(0)
    dv_copy_z.wait_recv()
    dvhat = s * (total + dv_z[...].astype(F32)).T
    vhat = film[...] * vnorm
    gv[...] = vnorm * (dvhat - vhat * jnp.sum(vhat * dvhat, axis=1, keepdims=True))

    gv_store = pltpu.make_async_copy(gv, gv_out, io_sem.at[1])
    gv_store.start()
    for copy in copies:
        if not any(copy is other for other in sent):
            copy.wait_send()
    gc_store.wait()
    gv_store.wait()


N_COPIES = 76


def hand_over(a, b, c, a_out, b_out, c_out, a_held, b_held, c_held, sem):
    held = (a_held, b_held, c_held)
    loads = [pltpu.make_async_copy(src, dst, sem.at[0, i]) for i, (src, dst) in enumerate(zip((a, b, c), held))]
    stores = [pltpu.make_async_copy(src, dst, sem.at[1, i]) for i, (src, dst) in enumerate(zip(held, (a_out, b_out, c_out)))]
    for load in loads:
        load.start()
    for load, store in zip(loads, stores):
        load.wait()
        store.start()
    for store in stores:
        store.wait()


def shards(film, text, matched, scale, shift):
    vmem = pl.BlockSpec(memory_space=pltpu.VMEM)
    hbm = pl.BlockSpec(memory_space=pltpu.HBM)
    loss, gv, gc = pl.pallas_call(
        kernel,
        out_shape=(
            jax.ShapeDtypeStruct((1, ROWS), F32),
            jax.ShapeDtypeStruct((ROWS, D), F32),
            jax.ShapeDtypeStruct((ROWS, D), F32),
        ),
        in_specs=[hbm] * 5,
        out_specs=(vmem, hbm, hbm),
        scratch_shapes=[
            pltpu.VMEM((ROWS, D), F32),
            pltpu.VMEM((ROWS, D), F32),
            pltpu.VMEM((ROWS, ROWS), jnp.int32),
            pltpu.SMEM((1,), F32),
            pltpu.SMEM((1,), F32),
            pltpu.VMEM((ROWS, D), F32),
            pltpu.VMEM((ROWS, D), F32),
            pltpu.VMEM((2048, D), BF16),
            pltpu.VMEM((1024, D), BF16),
            pltpu.VMEM((D, 1024), BF16),
            pltpu.VMEM((1024, 2048), BF16),
            pltpu.VMEM((8, 1024, 256), F32),
            pltpu.VMEM((8, 1, 256), jnp.int32),
            pltpu.SMEM((8,), jnp.int32),
            pltpu.VMEM((16, 8, ROWS), F32),
            pltpu.VMEM((8, D, ROWS), F32),
            pltpu.VMEM((8, D, ROWS), BF16),
            pltpu.VMEM((8, D, ROWS), BF16),
            pltpu.VMEM((8, D, ROWS), BF16),
            pltpu.VMEM((2, D, ROWS), BF16),
            pltpu.VMEM((4, D, ROWS), BF16),
            pltpu.VMEM((D, ROWS), BF16),
            pltpu.VMEM((D, ROWS), BF16),
            pltpu.VMEM((8, ROWS, D), F32),
            pltpu.VMEM((8, ROWS, D), BF16),
            pltpu.VMEM((2, ROWS, D), BF16),
            pltpu.VMEM((4, ROWS, D), BF16),
            pltpu.VMEM((ROWS, D), BF16),
            pltpu.VMEM((8, 8, ROWS), F32),
            pltpu.VMEM((6, 8, ROWS), F32),
            pltpu.VMEM((8, ROWS), F32),
            pltpu.SemaphoreType.DMA((N_COPIES,)),
            pltpu.SemaphoreType.DMA((N_COPIES,)),
            pltpu.SemaphoreType.DMA((5,)),
        ],
        compiler_params=pltpu.CompilerParams(
            collective_id=0, has_side_effects=True, vmem_limit_bytes=60 * 2**20
        ),
        cost_estimate=pl.CostEstimate(flops=13 * 10**9, bytes_accessed=2 * 2**20, transcendentals=0),
    )(film, text, matched.reshape(ROWS, ROWS), scale, shift)
    loss, gv, gc = pl.pallas_call(
        hand_over,
        out_shape=tuple(jax.ShapeDtypeStruct(a.shape, a.dtype) for a in (loss, gv, gc)),
        in_specs=[hbm] * 3,
        out_specs=(hbm,) * 3,
        scratch_shapes=[pltpu.VMEM(a.shape, a.dtype) for a in (loss, gv, gc)] + [pltpu.SemaphoreType.DMA((2, 3))],
    )(loss, gv, gc)
    return loss.reshape(ROWS), gv, gc


def solution(mesh):
    return jax.shard_map(
        shards,
        mesh=mesh,
        in_specs=(P(("row", "col"), None), P(("col", "row"), None), P(), P(), P()),
        out_specs=(P(("row", "col")), P(("row", "col"), None), P(("col", "row"), None)),
        check_vma=False,
    )
```

```python
import functools

import jax
import jax.numpy as jnp
from jax import lax
from jax.experimental import pallas as pl
from jax.experimental.pallas import tpu as pltpu
from jax.sharding import PartitionSpec as P

D = 1024
ROWS = 128
HALF = 64
CH = 32
LOG2E = 1.4426950408889634
LN2 = 0.6931471805599453
MESH = pl.DeviceIdType.MESH
F32 = jnp.float32
BF16 = jnp.bfloat16

RING = (0, 1, 3, 2)
OWN, NEXT, PREV, FAR = 0, 1, 2, 3


def position():
    r, c = lax.axis_index("row"), lax.axis_index("col")
    y, zl = r % 4, r // 4
    core, zh, x = c % 2, (c // 2) % 2, c // 4
    return r, c, x, y, zl, zh, core


def kernel(
    film_in, text_in, labels_in, scale_in, shift_in, loss_out, gv_out, gc_out,
    film, text, labels, scale, shift, gv, gc, v16, c16, ct, coef, logits, lab, base, losses,
    dv_own, dv_sib, dv_tx, dv_core, dv_far, dv_ring, dv_z, dv_ztx,
    dc, dc_tx, dc_far, dc_ring, dc_z,
    ls_core, ls_ring, ls_z, send_sem, recv_sem, io_sem,
):
    r, c, x, y, zl, zh, core = position()

    def dev(dx=0, dz_hi=0, dcore=0, dy=0, dz_lo=0):
        cc = (((x + dx) % 4) * 2 + (zh + dz_hi) % 2) * 2 + (core + dcore) % 2
        rr = ((zl + dz_lo) % 2) * 4 + (y + dy) % 4
        return (rr, cc)

    x_next, x_prev, x_far = dev(dx=1), dev(dx=3), dev(dx=2)
    y_next, y_prev = dev(dy=1), dev(dy=3)
    z_hi, z_lo, sibling = dev(dz_hi=1), dev(dz_lo=1), dev(dcore=1)

    barrier = pltpu.get_barrier_semaphore()
    peers = (x_next, x_prev, x_far, y_next, y_prev, z_hi, z_lo, sibling)
    for peer in peers:
        pl.semaphore_signal(barrier, inc=1, device_id=peer, device_id_type=MESH)

    loads = [
        pltpu.make_async_copy(src, dst, io_sem.at[i])
        for i, (src, dst) in enumerate((
            (film_in, film), (text_in, text), (labels_in, labels), (scale_in, scale), (shift_in, shift)
        ))
    ]
    for load in loads:
        load.start()

    copies, sent = [], []

    def send(src, dst, peer):
        i = len(copies)
        copy = pltpu.make_async_remote_copy(
            src_ref=src, dst_ref=dst, send_sem=send_sem.at[i], recv_sem=recv_sem.at[i],
            device_id=peer, device_id_type=MESH,
        )
        copies.append(copy)
        copy.start()
        return copy

    loads[0].wait()
    f = film[...]
    vnorm = lax.rsqrt(jnp.sum(f * f, axis=1, keepdims=True) + 1e-06)
    v16[0:ROWS, :] = (f * vnorm).astype(BF16)
    loads[1].wait()
    t = text[...]
    cnorm = lax.rsqrt(jnp.sum(t * t, axis=1, keepdims=True) + 1e-06)
    c16[0:ROWS, :] = (t * cnorm).astype(BF16)

    pl.semaphore_wait(barrier, len(peers))

    def vrow(slot, dk=0, lo=0, n=ROWS):
        return v16.at[pl.ds(slot * 2 * ROWS + dk * ROWS + lo, n), :]

    def crow(slot, lo=0, n=ROWS):
        return c16.at[pl.ds(slot * ROWS + lo, n), :]

    def gather_first(row, z, nxt, prv):
        return {
            "PA": send(row(4 * z, lo=0, n=HALF), row(4 * z + PREV, lo=0, n=HALF), nxt),
            "NB": send(row(4 * z, lo=HALF, n=HALF), row(4 * z + NEXT, lo=HALF, n=HALF), prv),
        }

    def gather_second(row, z, g, nxt, prv):
        g["PA"].wait_send()
        g["PB"] = send(row(4 * z, lo=HALF, n=HALF), row(4 * z + PREV, lo=HALF, n=HALF), nxt)
        g["NB"].wait_send()
        g["NA"] = send(row(4 * z, lo=0, n=HALF), row(4 * z + NEXT, lo=0, n=HALF), prv)
        sent.extend((g["PA"], g["NB"]))

    def forward(row, z, g, nxt, prv):
        g["PA"].wait_recv()
        g["FA"] = send(row(4 * z + PREV, lo=0, n=HALF), row(4 * z + FAR, lo=0, n=HALF), nxt)
        g["NB"].wait_recv()
        g["FB"] = send(row(4 * z + NEXT, lo=HALF, n=HALF), row(4 * z + FAR, lo=HALF, n=HALF), prv)

    core_copy = {}

    def to_sibling(slot):
        core_copy[slot] = send(vrow(slot), vrow(slot, dk=1), sibling)

    v_zh = send(vrow(0), vrow(4), z_hi)
    gv0 = gather_first(vrow, 0, x_next, x_prev)
    gc0 = gather_first(crow, 0, y_next, y_prev)
    to_sibling(0)

    for load in loads[2:]:
        load.wait()
    s = scale[0]
    b = shift[0]
    for p in range(8):
        dz, i = p // 4, p % 4
        for dk in range(2):
            block = r * 16 + (((x + RING[i]) % 4) * 2 + (zh + dz) % 2) * 2 + (core + dk) % 2
            lab[p, :, dk * ROWS : (dk + 1) * ROWS] = labels[pl.ds(block, 1), :]
        base[p] = (c * 8 + ((zl + dz) % 2) * 4 + (y + RING[i]) % 4) * ROWS
    losses[...] = jnp.zeros_like(losses)

    def transpose_c(slot):
        ct[:, slot * ROWS : (slot + 1) * ROWS] = c16[slot * ROWS : (slot + 1) * ROWS, :].T

    scale2 = s * LOG2E
    shift2 = b * LOG2E

    def act_many(p0, p1, q0, nq):
        left = c16[q0 * ROWS : (q0 + nq) * ROWS, :]
        for p in range(p0, p1):
            logits[p, 0 : nq * ROWS, :] = lax.dot_general(
                left, v16[p * 256 : (p + 1) * 256, :], (((1,), (1,)), ((), ())), preferred_element_type=F32
            )
        ids = lax.broadcasted_iota(jnp.int32, (CH, 256), 0)

        def pair(p, _):
            cols = pl.ds(pl.multiple_of(p * 256, 256), 256)

            def shard(k, acc):
                mine = lab[p] - base[q0 + k]
                for j in range(ROWS // CH):
                    sign = jnp.where((mine - j * CH) == ids, -1.0, 1.0).astype(F32)
                    rows = pl.ds(pl.multiple_of(k * ROWS + j * CH, CH), CH)
                    e = jnp.exp2((logits[p, rows, :] * scale2 + shift2) * sign)
                    w = 1.0 + e
                    inv = pltpu.reciprocal(w, full_range=False)
                    part = jnp.log2(w) * LN2 + (e - (w - 1.0)) * inv
                    coef[pl.ds(pl.multiple_of((q0 + k) * ROWS + j * CH, CH), CH), cols] = (
                        sign * (e * inv)
                    ).astype(BF16)
                    for i in range(CH // 8):
                        acc = acc + part[i * 8 : (i + 1) * 8, :]
                return acc

            acc = jnp.zeros((8, 256), F32)
            acc = shard(0, acc) if nq == 1 else lax.fori_loop(0, nq, shard, acc)
            losses[p] = losses[p] + acc[:, 0:ROWS]
            losses[8 + p] = losses[8 + p] + acc[:, ROWS:]
            return 0

        lax.fori_loop(p0, p1, pair, 0)

    dv_core_copy = {}

    def make_dv(p):
        for m in range(2):
            rows = slice(m * 512, (m + 1) * 512)
            out = jnp.dot(ct[rows, :], coef[:, p * 256 : (p + 1) * 256], preferred_element_type=F32)
            dv_own[p, rows, :] = out[:, 0:ROWS]
            dv_sib[p, rows, :] = out[:, ROWS:].astype(BF16)
        dv_core_copy[p] = send(dv_sib.at[p], dv_core.at[p], sibling)

    transpose_c(0)
    core_copy[0].wait_recv()
    act_many(0, 1, 0, 1)
    gather_second(vrow, 0, gv0, x_next, x_prev)
    gather_second(crow, 0, gc0, y_next, y_prev)
    forward(vrow, 0, gv0, x_next, x_prev)
    forward(crow, 0, gc0, y_next, y_prev)
    v_zh.wait_send()
    sent.append(v_zh)
    c_zl = send(crow(0), crow(4), z_lo)
    v_zh.wait_recv()
    gv1 = gather_first(vrow, 1, x_next, x_prev)
    to_sibling(4)
    gv0["NA"].wait_recv()
    to_sibling(NEXT)
    gv0["PB"].wait_recv()
    to_sibling(PREV)
    gc0["NA"].wait_recv()
    gc0["PB"].wait_recv()
    transpose_c(1)
    transpose_c(2)
    act_many(0, 1, 1, 2)
    core_copy[1].wait_recv()
    core_copy[2].wait_recv()
    act_many(1, 3, 0, 3)
    gather_second(vrow, 1, gv1, x_next, x_prev)
    gv0["FA"].wait_recv()
    gv0["FB"].wait_recv()
    to_sibling(FAR)
    gc0["FA"].wait_recv()
    gc0["FB"].wait_recv()
    transpose_c(3)
    act_many(0, 3, 3, 1)
    c_zl.wait_recv()
    gc1 = gather_first(crow, 1, y_next, y_prev)
    forward(vrow, 1, gv1, x_next, x_prev)
    core_copy[3].wait_recv()
    core_copy[4].wait_recv()
    act_many(3, 5, 0, 4)
    transpose_c(4)
    act_many(0, 5, 4, 1)
    gather_second(crow, 1, gc1, y_next, y_prev)
    gv1["NA"].wait_recv()
    to_sibling(4 + NEXT)
    gv1["PB"].wait_recv()
    to_sibling(4 + PREV)
    forward(crow, 1, gc1, y_next, y_prev)
    core_copy[5].wait_recv()
    core_copy[6].wait_recv()
    act_many(5, 7, 0, 5)
    gv1["FA"].wait_recv()
    gv1["FB"].wait_recv()
    to_sibling(4 + FAR)
    gc1["NA"].wait_recv()
    gc1["PB"].wait_recv()
    transpose_c(5)
    transpose_c(6)
    act_many(0, 7, 5, 2)
    core_copy[7].wait_recv()
    act_many(7, 8, 0, 7)
    gc1["FA"].wait_recv()
    gc1["FB"].wait_recv()
    transpose_c(7)
    act_many(7, 8, 7, 1)
    make_dv(7)
    act_many(0, 7, 7, 1)

    ls_copy_core = send(losses.at[pl.ds(8, 8)], ls_core, sibling)

    def make_dc(q):
        def body(n, _):
            cols = pl.ds(pl.multiple_of(n * 512, 512), 512)
            dc[q, :, cols] = jnp.dot(
                coef[q * ROWS : (q + 1) * ROWS, :], v16[:, cols], preferred_element_type=F32
            )
            return 0

        lax.fori_loop(0, 2, body, 0)

    dv_far_copy, dv_ring_copy, dc_far_copy, dc_ring_copy = {}, {}, {}, {}

    def dv_send_far(z):
        p = 4 * z + FAR
        dv_core_copy[p].wait_recv()
        dv_tx[p] = (dv_own[p] + dv_core[p].astype(F32)).astype(BF16)
        dv_far_copy[z, 0] = send(dv_tx.at[p, pl.ds(0, 512)], dv_far.at[z, pl.ds(0, 512)], x_next)
        dv_far_copy[z, 1] = send(dv_tx.at[p, pl.ds(512, 512)], dv_far.at[z, pl.ds(512, 512)], x_prev)

    def dv_send_free(z):
        for i, peer, k in ((NEXT, x_next, 1), (PREV, x_prev, 0)):
            p = 4 * z + i
            dv_core_copy[p].wait_recv()
            half = pl.ds(512 * k, 512)
            dv_tx[p, half, :] = (dv_own[p, half, :] + dv_core[p, half, :].astype(F32)).astype(BF16)
            dv_ring_copy[z, i, k] = send(dv_tx.at[p, half], dv_ring.at[2 * z + i - 1, half], peer)

    def dv_send_rest(z):
        for i, peer, k in ((NEXT, x_next, 0), (PREV, x_prev, 1)):
            p = 4 * z + i
            half = pl.ds(512 * k, 512)
            dv_far_copy[z, k].wait_recv()
            dv_tx[p, half, :] = (
                dv_own[p, half, :] + dv_core[p, half, :].astype(F32) + dv_far[z, half, :].astype(F32)
            ).astype(BF16)
            dv_ring_copy[z, i, k] = send(dv_tx.at[p, half], dv_ring.at[2 * z + i - 1, half], peer)

    def dv_total(z):
        p = 4 * z
        dv_core_copy[p].wait_recv()
        for i in (NEXT, PREV):
            for k in range(2):
                dv_ring_copy[z, i, k].wait_recv()
        return (
            dv_own[p] + dv_core[p].astype(F32)
            + (dv_ring[2 * z].astype(F32) + dv_ring[2 * z + 1].astype(F32))
        )

    def dc_send_far(z):
        q = 4 * z + FAR
        dc_tx[q] = dc[q].astype(BF16)
        dc_far_copy[z, 0] = send(dc_tx.at[q, pl.ds(0, HALF)], dc_far.at[z, pl.ds(0, HALF)], y_next)
        dc_far_copy[z, 1] = send(dc_tx.at[q, pl.ds(HALF, HALF)], dc_far.at[z, pl.ds(HALF, HALF)], y_prev)

    def dc_send_free(z):
        for i, peer, k in ((NEXT, y_next, 1), (PREV, y_prev, 0)):
            q = 4 * z + i
            half = pl.ds(HALF * k, HALF)
            dc_tx[q, half, :] = dc[q, half, :].astype(BF16)
            dc_ring_copy[z, i, k] = send(dc_tx.at[q, half], dc_ring.at[2 * z + i - 1, half], peer)

    def dc_send_rest(z):
        for i, peer, k in ((NEXT, y_next, 0), (PREV, y_prev, 1)):
            q = 4 * z + i
            half = pl.ds(HALF * k, HALF)
            dc_far_copy[z, k].wait_recv()
            dc_tx[q, half, :] = (dc[q, half, :] + dc_far[z, half, :].astype(F32)).astype(BF16)
            dc_ring_copy[z, i, k] = send(dc_tx.at[q, half], dc_ring.at[2 * z + i - 1, half], peer)

    def dc_total(z):
        for i in (NEXT, PREV):
            for k in range(2):
                dc_ring_copy[z, i, k].wait_recv()
        return dc[4 * z] + (dc_ring[2 * z].astype(F32) + dc_ring[2 * z + 1].astype(F32))

    dv_send_far(1)
    make_dc(7)
    dc_send_far(1)
    make_dv(5)
    make_dv(6)
    make_dc(5)
    make_dc(6)
    dc_send_free(1)
    dv_send_free(1)
    ls_copy_core.wait_recv()
    for p in range(8):
        losses[p] = losses[p] + ls_core[p]
    ls_copies = []
    for i, peer in ((NEXT, x_next), (PREV, x_prev), (FAR, x_far)):
        for z in range(2):
            ls_copies.append(send(losses.at[4 * z + i], ls_ring.at[3 * z + i - 1], peer))
    make_dc(4)
    make_dv(4)
    dc_send_rest(1)
    dv_send_rest(1)
    make_dc(3)
    make_dv(3)
    dc_send_far(0)
    make_dc(1)
    make_dc(2)
    dv_send_far(0)
    dc_tx[4] = dc_total(1).astype(BF16)
    dc_copy_z = send(dc_tx.at[4], dc_z, z_lo)
    dv_ztx[...] = dv_total(1).astype(BF16)
    dv_copy_z = send(dv_ztx, dv_z, z_hi)
    make_dv(1)
    make_dv(2)
    dc_send_free(0)
    dv_send_free(0)
    dc_send_rest(0)
    dv_send_rest(0)
    make_dc(0)
    make_dv(0)
    for copy in ls_copies:
        copy.wait_recv()
    losses[4] = losses[4] + (ls_ring[3] + ls_ring[4] + ls_ring[5])
    losses[0] = losses[0] + (ls_ring[0] + ls_ring[1] + ls_ring[2])
    ls_copy_z = send(losses.at[4], ls_z, z_hi)
    ls_copy_z.wait_recv()
    loss_out[...] = jnp.sum(losses[0] + ls_z[...], axis=0, keepdims=True)

    total = dc_total(0)
    dc_copy_z.wait_recv()
    dchat = s * (total + dc_z[...].astype(F32))
    chat = text[...] * cnorm
    gc[...] = cnorm * (dchat - chat * jnp.sum(chat * dchat, axis=1, keepdims=True))

    gc_store = pltpu.make_async_copy(gc, gc_out, io_sem.at[0])
    gc_store.start()

    total = dv_total(0)
    dv_copy_z.wait_recv()
    dvhat = s * (total + dv_z[...].astype(F32)).T
    vhat = film[...] * vnorm
    gv[...] = vnorm * (dvhat - vhat * jnp.sum(vhat * dvhat, axis=1, keepdims=True))

    gv_store = pltpu.make_async_copy(gv, gv_out, io_sem.at[1])
    gv_store.start()
    for copy in copies:
        if not any(copy is other for other in sent):
            copy.wait_send()
    gc_store.wait()
    gv_store.wait()


N_COPIES = 76


def hand_over(a, b, c, a_out, b_out, c_out, a_held, b_held, c_held, sem):
    held = (a_held, b_held, c_held)
    loads = [pltpu.make_async_copy(src, dst, sem.at[0, i]) for i, (src, dst) in enumerate(zip((a, b, c), held))]
    stores = [pltpu.make_async_copy(src, dst, sem.at[1, i]) for i, (src, dst) in enumerate(zip(held, (a_out, b_out, c_out)))]
    for load in loads:
        load.start()
    for load, store in zip(loads, stores):
        load.wait()
        store.start()
    for store in stores:
        store.wait()


def shards(film, text, matched, scale, shift):
    vmem = pl.BlockSpec(memory_space=pltpu.VMEM)
    hbm = pl.BlockSpec(memory_space=pltpu.HBM)
    loss, gv, gc = pl.pallas_call(
        kernel,
        out_shape=(
            jax.ShapeDtypeStruct((1, ROWS), F32),
            jax.ShapeDtypeStruct((ROWS, D), F32),
            jax.ShapeDtypeStruct((ROWS, D), F32),
        ),
        in_specs=[hbm] * 5,
        out_specs=(vmem, hbm, hbm),
        scratch_shapes=[
            pltpu.VMEM((ROWS, D), F32),
            pltpu.VMEM((ROWS, D), F32),
            pltpu.VMEM((ROWS, ROWS), jnp.int32),
            pltpu.SMEM((1,), F32),
            pltpu.SMEM((1,), F32),
            pltpu.VMEM((ROWS, D), F32),
            pltpu.VMEM((ROWS, D), F32),
            pltpu.VMEM((2048, D), BF16),
            pltpu.VMEM((1024, D), BF16),
            pltpu.VMEM((D, 1024), BF16),
            pltpu.VMEM((1024, 2048), BF16),
            pltpu.VMEM((8, 1024, 256), F32),
            pltpu.VMEM((8, 1, 256), jnp.int32),
            pltpu.SMEM((8,), jnp.int32),
            pltpu.VMEM((16, 8, ROWS), F32),
            pltpu.VMEM((8, D, ROWS), F32),
            pltpu.VMEM((8, D, ROWS), BF16),
            pltpu.VMEM((8, D, ROWS), BF16),
            pltpu.VMEM((8, D, ROWS), BF16),
            pltpu.VMEM((2, D, ROWS), BF16),
            pltpu.VMEM((4, D, ROWS), BF16),
            pltpu.VMEM((D, ROWS), BF16),
            pltpu.VMEM((D, ROWS), BF16),
            pltpu.VMEM((8, ROWS, D), F32),
            pltpu.VMEM((8, ROWS, D), BF16),
            pltpu.VMEM((2, ROWS, D), BF16),
            pltpu.VMEM((4, ROWS, D), BF16),
            pltpu.VMEM((ROWS, D), BF16),
            pltpu.VMEM((8, 8, ROWS), F32),
            pltpu.VMEM((6, 8, ROWS), F32),
            pltpu.VMEM((8, ROWS), F32),
            pltpu.SemaphoreType.DMA((N_COPIES,)),
            pltpu.SemaphoreType.DMA((N_COPIES,)),
            pltpu.SemaphoreType.DMA((5,)),
        ],
        compiler_params=pltpu.CompilerParams(
            collective_id=0, has_side_effects=True, vmem_limit_bytes=60 * 2**20
        ),
        cost_estimate=pl.CostEstimate(flops=13 * 10**9, bytes_accessed=2 * 2**20, transcendentals=0),
    )(film, text, matched.reshape(ROWS, ROWS), scale, shift)
    loss, gv, gc = pl.pallas_call(
        hand_over,
        out_shape=tuple(jax.ShapeDtypeStruct(a.shape, a.dtype) for a in (loss, gv, gc)),
        in_specs=[hbm] * 3,
        out_specs=(hbm,) * 3,
        scratch_shapes=[pltpu.VMEM(a.shape, a.dtype) for a in (loss, gv, gc)] + [pltpu.SemaphoreType.DMA((2, 3))],
    )(loss, gv, gc)
    return loss.reshape(ROWS), gv, gc


def solution(mesh):
    return jax.shard_map(
        shards,
        mesh=mesh,
        in_specs=(P(("row", "col"), None), P(("col", "row"), None), P(), P(), P()),
        out_specs=(P(("row", "col")), P(("row", "col"), None), P(("col", "row"), None)),
        check_vma=False,
    )
```

```python
import functools

import jax
import jax.numpy as jnp
from jax import lax
from jax.experimental import pallas as pl
from jax.experimental.pallas import tpu as pltpu
from jax.sharding import PartitionSpec as P

D = 1024
ROWS = 128
HALF = 64
CH = 64
LOG2E = 1.4426950408889634
LN2 = 0.6931471805599453
MESH = pl.DeviceIdType.MESH
F32 = jnp.float32
BF16 = jnp.bfloat16

RING = (0, 1, 3, 2)
OWN, NEXT, PREV, FAR = 0, 1, 2, 3


def position():
    r, c = lax.axis_index("row"), lax.axis_index("col")
    y, zl = r % 4, r // 4
    core, zh, x = c % 2, (c // 2) % 2, c // 4
    return r, c, x, y, zl, zh, core


def kernel(
    film_in, text_in, labels_in, scale_in, shift_in, loss_out, gv_out, gc_out,
    film, text, labels, scale, shift, gv, gc, v16, c16, ct, coef, logits, lab, base, losses,
    dv_own, dv_sib, dv_tx, dv_core, dv_far, dv_ring, dv_z, dv_ztx,
    dc, dc_tx, dc_far, dc_ring, dc_z,
    ls_core, ls_ring, ls_z, send_sem, recv_sem, io_sem,
):
    r, c, x, y, zl, zh, core = position()

    def dev(dx=0, dz_hi=0, dcore=0, dy=0, dz_lo=0):
        cc = (((x + dx) % 4) * 2 + (zh + dz_hi) % 2) * 2 + (core + dcore) % 2
        rr = ((zl + dz_lo) % 2) * 4 + (y + dy) % 4
        return (rr, cc)

    x_next, x_prev, x_far = dev(dx=1), dev(dx=3), dev(dx=2)
    y_next, y_prev = dev(dy=1), dev(dy=3)
    z_hi, z_lo, sibling = dev(dz_hi=1), dev(dz_lo=1), dev(dcore=1)

    barrier = pltpu.get_barrier_semaphore()
    peers = (x_next, x_prev, x_far, y_next, y_prev, z_hi, z_lo, sibling)
    for peer in peers:
        pl.semaphore_signal(barrier, inc=1, device_id=peer, device_id_type=MESH)

    loads = [
        pltpu.make_async_copy(src, dst, io_sem.at[i])
        for i, (src, dst) in enumerate((
            (film_in, film), (text_in, text), (labels_in, labels), (scale_in, scale), (shift_in, shift)
        ))
    ]
    for load in loads:
        load.start()

    copies, sent = [], []

    def send(src, dst, peer):
        i = len(copies)
        copy = pltpu.make_async_remote_copy(
            src_ref=src, dst_ref=dst, send_sem=send_sem.at[i], recv_sem=recv_sem.at[i],
            device_id=peer, device_id_type=MESH,
        )
        copies.append(copy)
        copy.start()
        return copy

    loads[0].wait()
    f = film[...]
    vnorm = lax.rsqrt(jnp.sum(f * f, axis=1, keepdims=True) + 1e-06)
    v16[0:ROWS, :] = (f * vnorm).astype(BF16)
    loads[1].wait()
    t = text[...]
    cnorm = lax.rsqrt(jnp.sum(t * t, axis=1, keepdims=True) + 1e-06)
    c16[0:ROWS, :] = (t * cnorm).astype(BF16)

    pl.semaphore_wait(barrier, len(peers))

    def vrow(slot, dk=0, lo=0, n=ROWS):
        return v16.at[pl.ds(slot * 2 * ROWS + dk * ROWS + lo, n), :]

    def crow(slot, lo=0, n=ROWS):
        return c16.at[pl.ds(slot * ROWS + lo, n), :]

    def gather_first(row, z, nxt, prv):
        return {
            "PA": send(row(4 * z, lo=0, n=HALF), row(4 * z + PREV, lo=0, n=HALF), nxt),
            "NB": send(row(4 * z, lo=HALF, n=HALF), row(4 * z + NEXT, lo=HALF, n=HALF), prv),
        }

    def gather_second(row, z, g, nxt, prv):
        g["PA"].wait_send()
        g["PB"] = send(row(4 * z, lo=HALF, n=HALF), row(4 * z + PREV, lo=HALF, n=HALF), nxt)
        g["NB"].wait_send()
        g["NA"] = send(row(4 * z, lo=0, n=HALF), row(4 * z + NEXT, lo=0, n=HALF), prv)
        sent.extend((g["PA"], g["NB"]))

    def forward(row, z, g, nxt, prv):
        g["PA"].wait_recv()
        g["FA"] = send(row(4 * z + PREV, lo=0, n=HALF), row(4 * z + FAR, lo=0, n=HALF), nxt)
        g["NB"].wait_recv()
        g["FB"] = send(row(4 * z + NEXT, lo=HALF, n=HALF), row(4 * z + FAR, lo=HALF, n=HALF), prv)

    core_copy = {}

    def to_sibling(slot):
        core_copy[slot] = send(vrow(slot), vrow(slot, dk=1), sibling)

    v_zh = send(vrow(0), vrow(4), z_hi)
    gv0 = gather_first(vrow, 0, x_next, x_prev)
    gc0 = gather_first(crow, 0, y_next, y_prev)
    to_sibling(0)

    for load in loads[2:]:
        load.wait()
    s = scale[0]
    b = shift[0]
    for p in range(8):
        dz, i = p // 4, p % 4
        for dk in range(2):
            block = r * 16 + (((x + RING[i]) % 4) * 2 + (zh + dz) % 2) * 2 + (core + dk) % 2
            lab[p, :, dk * ROWS : (dk + 1) * ROWS] = labels[pl.ds(block, 1), :]
        base[p] = (c * 8 + ((zl + dz) % 2) * 4 + (y + RING[i]) % 4) * ROWS
    losses[...] = jnp.zeros_like(losses)

    def transpose_c(slot):
        ct[:, slot * ROWS : (slot + 1) * ROWS] = c16[slot * ROWS : (slot + 1) * ROWS, :].T

    scale2 = s * LOG2E
    shift2 = b * LOG2E

    def act_many(p0, p1, q0, nq):
        left = c16[q0 * ROWS : (q0 + nq) * ROWS, :]
        for p in range(p0, p1):
            logits[p, 0 : nq * ROWS, :] = lax.dot_general(
                left, v16[p * 256 : (p + 1) * 256, :], (((1,), (1,)), ((), ())), preferred_element_type=F32
            )
        ids = lax.broadcasted_iota(jnp.int32, (CH, 256), 0)

        def pair(p, _):
            cols = pl.ds(pl.multiple_of(p * 256, 256), 256)

            def shard(k, acc):
                mine = lab[p] - base[q0 + k]
                for j in range(ROWS // CH):
                    sign = jnp.where((mine - j * CH) == ids, -1.0, 1.0).astype(F32)
                    rows = pl.ds(pl.multiple_of(k * ROWS + j * CH, CH), CH)
                    e = jnp.exp2((logits[p, rows, :] * scale2 + shift2) * sign)
                    w = 1.0 + e
                    inv = pltpu.reciprocal(w, full_range=False)
                    part = jnp.log2(w) * LN2 + (e - (w - 1.0)) * inv
                    coef[pl.ds(pl.multiple_of((q0 + k) * ROWS + j * CH, CH), CH), cols] = (
                        sign * (e * inv)
                    ).astype(BF16)
                    for i in range(CH // 8):
                        acc = acc + part[i * 8 : (i + 1) * 8, :]
                return acc

            acc = jnp.zeros((8, 256), F32)
            acc = shard(0, acc) if nq == 1 else lax.fori_loop(0, nq, shard, acc)
            losses[p] = losses[p] + acc[:, 0:ROWS]
            losses[8 + p] = losses[8 + p] + acc[:, ROWS:]
            return 0

        lax.fori_loop(p0, p1, pair, 0)

    dv_core_copy = {}

    def make_dv(p):
        for m in range(2):
            rows = slice(m * 512, (m + 1) * 512)
            out = jnp.dot(ct[rows, :], coef[:, p * 256 : (p + 1) * 256], preferred_element_type=F32)
            dv_own[p, rows, :] = out[:, 0:ROWS]
            dv_sib[p, rows, :] = out[:, ROWS:].astype(BF16)
        dv_core_copy[p] = send(dv_sib.at[p], dv_core.at[p], sibling)

    transpose_c(0)
    core_copy[0].wait_recv()
    act_many(0, 1, 0, 1)
    gather_second(vrow, 0, gv0, x_next, x_prev)
    gather_second(crow, 0, gc0, y_next, y_prev)
    forward(vrow, 0, gv0, x_next, x_prev)
    forward(crow, 0, gc0, y_next, y_prev)
    v_zh.wait_send()
    sent.append(v_zh)
    c_zl = send(crow(0), crow(4), z_lo)
    v_zh.wait_recv()
    gv1 = gather_first(vrow, 1, x_next, x_prev)
    to_sibling(4)
    gv0["NA"].wait_recv()
    to_sibling(NEXT)
    gv0["PB"].wait_recv()
    to_sibling(PREV)
    gc0["NA"].wait_recv()
    gc0["PB"].wait_recv()
    transpose_c(1)
    transpose_c(2)
    act_many(0, 1, 1, 2)
    core_copy[1].wait_recv()
    core_copy[2].wait_recv()
    act_many(1, 3, 0, 3)
    gather_second(vrow, 1, gv1, x_next, x_prev)
    gv0["FA"].wait_recv()
    gv0["FB"].wait_recv()
    to_sibling(FAR)
    gc0["FA"].wait_recv()
    gc0["FB"].wait_recv()
    transpose_c(3)
    act_many(0, 3, 3, 1)
    forward(vrow, 1, gv1, x_next, x_prev)
    c_zl.wait_recv()
    gc1 = gather_first(crow, 1, y_next, y_prev)
    core_copy[3].wait_recv()
    core_copy[4].wait_recv()
    act_many(3, 5, 0, 4)
    gather_second(crow, 1, gc1, y_next, y_prev)
    gv1["NA"].wait_recv()
    to_sibling(4 + NEXT)
    gv1["PB"].wait_recv()
    to_sibling(4 + PREV)
    transpose_c(4)
    act_many(0, 5, 4, 1)
    forward(crow, 1, gc1, y_next, y_prev)
    core_copy[5].wait_recv()
    core_copy[6].wait_recv()
    act_many(5, 7, 0, 5)
    gv1["FA"].wait_recv()
    gv1["FB"].wait_recv()
    to_sibling(4 + FAR)
    gc1["NA"].wait_recv()
    gc1["PB"].wait_recv()
    transpose_c(5)
    transpose_c(6)
    act_many(0, 7, 5, 2)
    core_copy[7].wait_recv()
    act_many(7, 8, 0, 7)
    gc1["FA"].wait_recv()
    gc1["FB"].wait_recv()
    transpose_c(7)
    act_many(7, 8, 7, 1)
    make_dv(7)
    act_many(0, 7, 7, 1)

    ls_copy_core = send(losses.at[pl.ds(8, 8)], ls_core, sibling)

    def make_dc(q):
        def body(n, _):
            cols = pl.ds(pl.multiple_of(n * 512, 512), 512)
            dc[q, :, cols] = jnp.dot(
                coef[q * ROWS : (q + 1) * ROWS, :], v16[:, cols], preferred_element_type=F32
            )
            return 0

        lax.fori_loop(0, 2, body, 0)

    dv_far_copy, dv_ring_copy, dc_far_copy, dc_ring_copy = {}, {}, {}, {}

    def dv_send_far(z):
        p = 4 * z + FAR
        dv_core_copy[p].wait_recv()
        dv_tx[p] = (dv_own[p] + dv_core[p].astype(F32)).astype(BF16)
        dv_far_copy[z, 0] = send(dv_tx.at[p, pl.ds(0, 512)], dv_far.at[z, pl.ds(0, 512)], x_next)
        dv_far_copy[z, 1] = send(dv_tx.at[p, pl.ds(512, 512)], dv_far.at[z, pl.ds(512, 512)], x_prev)

    def dv_send_free(z):
        for i, peer, k in ((NEXT, x_next, 1), (PREV, x_prev, 0)):
            p = 4 * z + i
            dv_core_copy[p].wait_recv()
            half = pl.ds(512 * k, 512)
            dv_tx[p, half, :] = (dv_own[p, half, :] + dv_core[p, half, :].astype(F32)).astype(BF16)
            dv_ring_copy[z, i, k] = send(dv_tx.at[p, half], dv_ring.at[2 * z + i - 1, half], peer)

    def dv_send_rest(z):
        for i, peer, k in ((NEXT, x_next, 0), (PREV, x_prev, 1)):
            p = 4 * z + i
            half = pl.ds(512 * k, 512)
            dv_far_copy[z, k].wait_recv()
            dv_tx[p, half, :] = (
                dv_own[p, half, :] + dv_core[p, half, :].astype(F32) + dv_far[z, half, :].astype(F32)
            ).astype(BF16)
            dv_ring_copy[z, i, k] = send(dv_tx.at[p, half], dv_ring.at[2 * z + i - 1, half], peer)

    def dv_total(z):
        p = 4 * z
        dv_core_copy[p].wait_recv()
        for i in (NEXT, PREV):
            for k in range(2):
                dv_ring_copy[z, i, k].wait_recv()
        return (
            dv_own[p] + dv_core[p].astype(F32)
            + (dv_ring[2 * z].astype(F32) + dv_ring[2 * z + 1].astype(F32))
        )

    def dc_send_far(z):
        q = 4 * z + FAR
        dc_tx[q] = dc[q].astype(BF16)
        dc_far_copy[z, 0] = send(dc_tx.at[q, pl.ds(0, HALF)], dc_far.at[z, pl.ds(0, HALF)], y_next)
        dc_far_copy[z, 1] = send(dc_tx.at[q, pl.ds(HALF, HALF)], dc_far.at[z, pl.ds(HALF, HALF)], y_prev)

    def dc_send_free(z):
        for i, peer, k in ((NEXT, y_next, 1), (PREV, y_prev, 0)):
            q = 4 * z + i
            half = pl.ds(HALF * k, HALF)
            dc_tx[q, half, :] = dc[q, half, :].astype(BF16)
            dc_ring_copy[z, i, k] = send(dc_tx.at[q, half], dc_ring.at[2 * z + i - 1, half], peer)

    def dc_send_rest(z):
        for i, peer, k in ((NEXT, y_next, 0), (PREV, y_prev, 1)):
            q = 4 * z + i
            half = pl.ds(HALF * k, HALF)
            dc_far_copy[z, k].wait_recv()
            dc_tx[q, half, :] = (dc[q, half, :] + dc_far[z, half, :].astype(F32)).astype(BF16)
            dc_ring_copy[z, i, k] = send(dc_tx.at[q, half], dc_ring.at[2 * z + i - 1, half], peer)

    def dc_total(z):
        for i in (NEXT, PREV):
            for k in range(2):
                dc_ring_copy[z, i, k].wait_recv()
        return dc[4 * z] + (dc_ring[2 * z].astype(F32) + dc_ring[2 * z + 1].astype(F32))

    dv_send_far(1)
    make_dc(7)
    dc_send_far(1)
    make_dv(5)
    make_dv(6)
    make_dc(5)
    make_dc(6)
    dc_send_free(1)
    dv_send_free(1)
    ls_copy_core.wait_recv()
    for p in range(8):
        losses[p] = losses[p] + ls_core[p]
    ls_copies = []
    for i, peer in ((NEXT, x_next), (PREV, x_prev), (FAR, x_far)):
        for z in range(2):
            ls_copies.append(send(losses.at[4 * z + i], ls_ring.at[3 * z + i - 1], peer))
    make_dc(4)
    make_dv(4)
    dc_send_rest(1)
    dv_send_rest(1)
    make_dc(3)
    make_dv(3)
    dc_send_far(0)
    make_dc(1)
    make_dc(2)
    dv_send_far(0)
    dc_tx[4] = dc_total(1).astype(BF16)
    dc_copy_z = send(dc_tx.at[4], dc_z, z_lo)
    dv_ztx[...] = dv_total(1).astype(BF16)
    dv_copy_z = send(dv_ztx, dv_z, z_hi)
    make_dv(1)
    make_dv(2)
    dc_send_free(0)
    dv_send_free(0)
    dc_send_rest(0)
    dv_send_rest(0)
    make_dc(0)
    make_dv(0)
    for copy in ls_copies:
        copy.wait_recv()
    losses[4] = losses[4] + (ls_ring[3] + ls_ring[4] + ls_ring[5])
    losses[0] = losses[0] + (ls_ring[0] + ls_ring[1] + ls_ring[2])
    ls_copy_z = send(losses.at[4], ls_z, z_hi)
    ls_copy_z.wait_recv()
    loss_out[...] = jnp.sum(losses[0] + ls_z[...], axis=0, keepdims=True)

    total = dc_total(0)
    dc_copy_z.wait_recv()
    dchat = s * (total + dc_z[...].astype(F32))
    chat = text[...] * cnorm
    gc[...] = cnorm * (dchat - chat * jnp.sum(chat * dchat, axis=1, keepdims=True))

    gc_store = pltpu.make_async_copy(gc, gc_out, io_sem.at[0])
    gc_store.start()

    total = dv_total(0)
    dv_copy_z.wait_recv()
    dvhat = s * (total + dv_z[...].astype(F32)).T
    vhat = film[...] * vnorm
    gv[...] = vnorm * (dvhat - vhat * jnp.sum(vhat * dvhat, axis=1, keepdims=True))

    gv_store = pltpu.make_async_copy(gv, gv_out, io_sem.at[1])
    gv_store.start()
    for copy in copies:
        if not any(copy is other for other in sent):
            copy.wait_send()
    gc_store.wait()
    gv_store.wait()


N_COPIES = 76


def hand_over(a, b, c, a_out, b_out, c_out, a_held, b_held, c_held, sem):
    held = (a_held, b_held, c_held)
    loads = [pltpu.make_async_copy(src, dst, sem.at[0, i]) for i, (src, dst) in enumerate(zip((a, b, c), held))]
    stores = [pltpu.make_async_copy(src, dst, sem.at[1, i]) for i, (src, dst) in enumerate(zip(held, (a_out, b_out, c_out)))]
    for load in loads:
        load.start()
    for load, store in zip(loads, stores):
        load.wait()
        store.start()
    for store in stores:
        store.wait()


def shards(film, text, matched, scale, shift):
    vmem = pl.BlockSpec(memory_space=pltpu.VMEM)
    hbm = pl.BlockSpec(memory_space=pltpu.HBM)
    loss, gv, gc = pl.pallas_call(
        kernel,
        out_shape=(
            jax.ShapeDtypeStruct((1, ROWS), F32),
            jax.ShapeDtypeStruct((ROWS, D), F32),
            jax.ShapeDtypeStruct((ROWS, D), F32),
        ),
        in_specs=[hbm] * 5,
        out_specs=(vmem, hbm, hbm),
        scratch_shapes=[
            pltpu.VMEM((ROWS, D), F32),
            pltpu.VMEM((ROWS, D), F32),
            pltpu.VMEM((ROWS, ROWS), jnp.int32),
            pltpu.SMEM((1,), F32),
            pltpu.SMEM((1,), F32),
            pltpu.VMEM((ROWS, D), F32),
            pltpu.VMEM((ROWS, D), F32),
            pltpu.VMEM((2048, D), BF16),
            pltpu.VMEM((1024, D), BF16),
            pltpu.VMEM((D, 1024), BF16),
            pltpu.VMEM((1024, 2048), BF16),
            pltpu.VMEM((8, 1024, 256), F32),
            pltpu.VMEM((8, 1, 256), jnp.int32),
            pltpu.SMEM((8,), jnp.int32),
            pltpu.VMEM((16, 8, ROWS), F32),
            pltpu.VMEM((8, D, ROWS), F32),
            pltpu.VMEM((8, D, ROWS), BF16),
            pltpu.VMEM((8, D, ROWS), BF16),
            pltpu.VMEM((8, D, ROWS), BF16),
            pltpu.VMEM((2, D, ROWS), BF16),
            pltpu.VMEM((4, D, ROWS), BF16),
            pltpu.VMEM((D, ROWS), BF16),
            pltpu.VMEM((D, ROWS), BF16),
            pltpu.VMEM((8, ROWS, D), F32),
            pltpu.VMEM((8, ROWS, D), BF16),
            pltpu.VMEM((2, ROWS, D), BF16),
            pltpu.VMEM((4, ROWS, D), BF16),
            pltpu.VMEM((ROWS, D), BF16),
            pltpu.VMEM((8, 8, ROWS), F32),
            pltpu.VMEM((6, 8, ROWS), F32),
            pltpu.VMEM((8, ROWS), F32),
            pltpu.SemaphoreType.DMA((N_COPIES,)),
            pltpu.SemaphoreType.DMA((N_COPIES,)),
            pltpu.SemaphoreType.DMA((5,)),
        ],
        compiler_params=pltpu.CompilerParams(
            collective_id=0, has_side_effects=True, vmem_limit_bytes=60 * 2**20
        ),
        cost_estimate=pl.CostEstimate(flops=13 * 10**9, bytes_accessed=2 * 2**20, transcendentals=0),
    )(film, text, matched.reshape(ROWS, ROWS), scale, shift)
    loss, gv, gc = pl.pallas_call(
        hand_over,
        out_shape=tuple(jax.ShapeDtypeStruct(a.shape, a.dtype) for a in (loss, gv, gc)),
        in_specs=[hbm] * 3,
        out_specs=(hbm,) * 3,
        scratch_shapes=[pltpu.VMEM(a.shape, a.dtype) for a in (loss, gv, gc)] + [pltpu.SemaphoreType.DMA((2, 3))],
    )(loss, gv, gc)
    return loss.reshape(ROWS), gv, gc


def solution(mesh):
    return jax.shard_map(
        shards,
        mesh=mesh,
        in_specs=(P(("row", "col"), None), P(("col", "row"), None), P(), P(), P()),
        out_specs=(P(("row", "col")), P(("row", "col"), None), P(("col", "row"), None)),
        check_vma=False,
    )
```
